32 devices in a mesh: dp: 4 (over z), mp: 8 (over y, x, core).
Axes of the slice: x: 2, y: 2, z: 4, core: 2. Of those that a mesh axis runs over, the one named last changes fastest.
Arguments:
- stream: bfloat16 [16384, 2048], P(('dp', 'mp')), may hold values from -5.5 to 5.5
- norm_weight: float32 [2048], replicated, may hold values from 0.5 to 1.5
- query_key_weight: bfloat16 [2048, 512], P(('dp', 'mp')), may hold values from -0.25 to 0.25
- value_weight: bfloat16 [2048, 2048], P(('dp', 'mp')), may hold values from -0.125 to 0.125
- output_weight: bfloat16 [2048, 2048], P(('dp', 'mp')), may hold values from -0.5 to 0.5
- convolution_weights: float32 [3, 2048], replicated, may hold values from -2.5 to 2.5
- adapter_down_maps: bfloat16 [32, 16, 2048], P('mp'), may hold values from -0.125 to 0.125
- adapter_up_maps: bfloat16 [32, 16, 2048], P('mp'), may hold values from -1.5 to 1.5
- prompt_lengths: int32 [32, 8], P(('dp', 'mp')), may hold values from 1 to 256, 512 in all within a row
- block_adapter_index: int32 [512], P(('dp', 'mp')), may hold values from 0 to 31, as said below
Outputs:
- hidden: bfloat16 [16384, 2048], P(('dp', 'mp'))
The draws below stay inside these ranges and needn't reach their ends.
Inputs may be any that keep to these rules, and one draw needn't show every extreme that they name: `prompt_lengths`: each row holds the lengths of one device's 8 prompts; a row sums to 512 and its largest entry is exactly 256. `block_adapter_index`: adapters k * 4 to (k + 1) * 4 - 1 sit on index k of mp. The 16 blocks of one device name adapters of any one index of mp at most 4 times; in every draw, on each index of dp, one index of mp is named exactly 4 times by every device.
All inputs are finite; a program needn't handle non-finite values.
Results may differ from the reference program's by a relative error of at most 0.0088.
Values may be sent and summed in bfloat16 or wider, within the bound.
No kernel may reach another device: no remote copies, remote signals or barrier semaphores. Data moves between devices by JAX's collectives and lax.ppermute only.
A program may use at most 128 MiB of HBM per device.

```python
import math
import jax
import jax.numpy as jnp
import numpy as np
from jax import lax

MODEL_WIDTH = 2048
HEADS = 16
QK = 16
ADAPTER_RANK = 16
KERNEL = 3
PROMPTS = 8
BLK = 32
ADP_DEV = 4
TOK_DEV = 512
ADAPTER_COUNT = 32
TOKENS = 16384
BLK_DEV = 16
NBLK = 512
MOST = 4
MOST_LEN = 256
N_DP = 4
N_MP = 8
DEVICES = 32


def draw_stream(key, part):
    key_base, key_rows, key_cols = jax.random.split(key, 3)
    row_scale = jnp.exp(jax.random.uniform(key_rows, (TOKENS, 1), jnp.float32, math.log(0.1), 0.0))
    base = jnp.clip(jax.random.normal(key_base, (TOKENS, MODEL_WIDTH), jnp.float32), -6.0, 6.0)
    col_scale = jnp.exp(jax.random.uniform(key_cols, (1, MODEL_WIDTH), jnp.float32, math.log(0.3), math.log(3.0)))
    return (0.3 * base * row_scale * col_scale).astype(jnp.bfloat16)


def draw_block_adapter_index(key, part):
    key_hot, key_pick, key_sub = jax.random.split(jax.random.fold_in(key, 17), 3)
    hot_group = jax.random.randint(key_hot, (N_DP,), 0, N_MP)
    hot_device = jnp.repeat(hot_group, N_MP)
    leftover = jnp.arange(MOST, N_MP * MOST, dtype=jnp.int32) // MOST

    def one_device(device_key, hot_one):
        key_choose, key_place = jax.random.split(device_key, 2)
        chosen = jax.random.permutation(key_choose, leftover)[:BLK_DEV - MOST]
        relative = jnp.concatenate([jnp.zeros((MOST,), jnp.int32), chosen])
        relative = jax.random.permutation(key_place, relative)
        return (relative + hot_one) % N_MP
    device_keys = jax.random.split(key_pick, DEVICES)
    holder = jax.vmap(one_device)(device_keys, hot_device).reshape(NBLK)
    within = jax.random.randint(key_sub, (NBLK,), 0, ADP_DEV)
    return (holder * ADP_DEV + within).astype(jnp.int32)


def levels(rng, shape, shards, smallest, high):
    loudness = 1.0
    for dim, parts in shards:
        draws = jax.random.uniform(jax.random.fold_in(jax.random.fold_in(rng, 6), dim), (parts,), jnp.float32, smallest / len(shards), high / len(shards))
        loudness = loudness * jnp.repeat(jnp.exp(draws), shape[dim] // parts).reshape((-1,) + (1,) * (len(shape) - 1 - dim))
    return loudness


def split_up(count, total, bound, lean):
    portions = [(1 << 20) // math.isqrt(grade ** lean) + 1 for grade in range(2, count + 1)]
    rest, counts = total - bound - (count - 1), [1] * (count - 1)
    while rest > 0:
        free = [i for i in range(count - 1) if counts[i] < bound]
        pool, remaining = sum([portions[i] for i in free]), rest
        for i in free:
            addition = min(bound - counts[i], max(1, remaining * portions[i] // pool), rest)
            counts[i] = counts[i] + addition
            rest = rest - addition
    return np.array([bound] + counts)


def ragged_sizes(stream_key, amount, total, limit, lean):
    if amount == 2:
        one = jax.random.randint(stream_key, (), max(1, total - limit), min(limit, total - 1) + 1)
        return jnp.stack([one, total - one])
    tallies = jnp.asarray(split_up(amount, total, limit, lean), jnp.int32)
    couples = (amount - 1) // 2
    donor, taker = tallies[1:1 + 2 * couples:2], tallies[2:2 + 2 * couples:2]
    slack = jnp.minimum(donor - 1, limit - taker)
    passed = jax.random.randint(jax.random.fold_in(stream_key, 1), (couples,), 0, 1 << 20) % (slack + 1)
    tallies = tallies.at[1:1 + 2 * couples:2].set(donor - passed).at[2:2 + 2 * couples:2].set(taker + passed)
    return tallies[jax.random.permutation(jax.random.fold_in(stream_key, 2), amount)]


def scatter_about(stream_key, extent, scale, most, shards=(), kind=jnp.bfloat16):
    array = jax.random.normal(stream_key, extent, jnp.float32) * scale
    if len(shards) > 0:
        array = levels(stream_key, extent, shards, -0.22, 0.18) * array
    return jnp.clip(array, min=-most, max=most).astype(kind)


def setup_inputs(seed: int = 0) -> dict:
    arg_keys = jax.random.split(jax.random.key(seed), 11)
    stream = draw_stream(jax.random.fold_in(arg_keys[10], 71), 0)
    norm_weight = jnp.clip(1.0 + 0.1 * jax.random.normal(arg_keys[1], (MODEL_WIDTH,), jnp.float32), 0.5, 1.5)
    query_key_weight = scatter_about(arg_keys[2], (MODEL_WIDTH, 2 * HEADS * QK), (MODEL_WIDTH // 4) ** -0.5, 0.25, ((0, 32),))
    value_weight = scatter_about(arg_keys[3], (MODEL_WIDTH, MODEL_WIDTH), MODEL_WIDTH ** -0.5, 0.125, ((0, 32),))
    output_weight = scatter_about(arg_keys[4], (MODEL_WIDTH, MODEL_WIDTH), (MODEL_WIDTH // 16) ** -0.5, 0.5, ((0, 32),))
    convolution_weights = scatter_about(arg_keys[5], (KERNEL, MODEL_WIDTH), 0.5, 2.5, (), jnp.float32)
    adapter_down_maps = scatter_about(arg_keys[6], (ADAPTER_COUNT, ADAPTER_RANK, MODEL_WIDTH), MODEL_WIDTH ** -0.5, 0.125, ((0, 8),))
    adapter_up_maps = scatter_about(arg_keys[7], (ADAPTER_COUNT, ADAPTER_RANK, MODEL_WIDTH), ADAPTER_RANK ** -0.5, 1.5, ((0, 8),))
    prompt_lengths = jax.vmap(lambda own: ragged_sizes(own, PROMPTS, TOK_DEV, MOST_LEN, 2))(jax.random.split(arg_keys[8], DEVICES)).reshape((DEVICES, PROMPTS)).astype(jnp.int32)
    block_adapter_index = draw_block_adapter_index(jax.random.fold_in(arg_keys[10], 71), 0)
    return {"stream": stream, "norm_weight": norm_weight, "query_key_weight": query_key_weight, "value_weight": value_weight, "output_weight": output_weight, "convolution_weights": convolution_weights, "adapter_down_maps": adapter_down_maps, "adapter_up_maps": adapter_up_maps, "prompt_lengths": prompt_lengths, "block_adapter_index": block_adapter_index}


adapter_scale = 2.0
norm_eps = 1e-05

def prompt_index(lengths, total_token_count):
    bounds = jnp.cumsum(lengths)
    position = jnp.arange(total_token_count, dtype=jnp.int32)
    return lax.optimization_barrier(jnp.sum((position[:, None] >= bounds[None, :]).astype(jnp.int32), axis=1))

def short_conv(value_matrix, tap_table, segment):
    result = tap_table[0][None, :] * value_matrix
    for offset in range(1, tap_table.shape[0]):
        earlier = jnp.concatenate([jnp.zeros((offset, value_matrix.shape[1]), jnp.float32), value_matrix[:-offset]], axis=0)
        same_prompt = jnp.concatenate([jnp.zeros((offset,), jnp.bool_), segment[offset:] == segment[:-offset]], axis=0)
        result = result + tap_table[offset][None, :] * jnp.where(same_prompt[:, None], earlier, 0.0)
    return result

def taylor_heads(query_key, mixed, segment, head_count, feature):
    total_token_count, hidden_width = mixed.shape
    head_width = hidden_width // head_count
    queries = query_key[:, :head_count * feature].reshape(total_token_count, head_count, feature).transpose(1, 0, 2)
    key_rows = query_key[:, head_count * feature:].reshape(total_token_count, head_count, feature).transpose(1, 0, 2)
    value_rows = mixed.reshape(total_token_count, head_count, head_width).transpose(1, 0, 2)
    position = jnp.arange(total_token_count, dtype=jnp.int32)
    allowed = (position[None, :] <= position[:, None]) & (segment[None, :] == segment[:, None])
    score_scale = 1.0 / math.sqrt(feature)

    def one_head(operands):
        query_one, key_one, value_one = operands
        scores = jnp.dot(query_one, key_one.T, preferred_element_type=jnp.float32) * score_scale
        weight = jnp.where(allowed, 1.0 + scores + 0.5 * scores * scores, 0.0)
        row_total = lax.optimization_barrier(jnp.sum(weight, axis=1, keepdims=True))
        numerator = jnp.dot(weight.astype(jnp.bfloat16), value_one, preferred_element_type=jnp.float32)
        return numerator / row_total
    outputs = lax.map(one_head, (queries, key_rows, value_rows))
    return outputs.transpose(1, 0, 2).reshape(total_token_count, hidden_width).astype(jnp.bfloat16)

def reference(stream, norm_weight, query_key_weight, value_weight, output_weight, convolution_weights, adapter_down_maps, adapter_up_maps, prompt_lengths, block_adapter_index):
    flattened_down = adapter_down_maps.reshape(ADAPTER_COUNT * ADAPTER_RANK, MODEL_WIDTH)
    flattened_up = adapter_up_maps.reshape(ADAPTER_COUNT * ADAPTER_RANK, MODEL_WIDTH)
    owner = jnp.arange(ADAPTER_COUNT * ADAPTER_RANK, dtype=jnp.int32) // ADAPTER_RANK

    def device_layer(operands):
        rows_in, lengths, adapters = operands
        stream_f = rows_in.astype(jnp.float32)
        mean_sq = lax.optimization_barrier(jnp.mean(stream_f * stream_f, axis=1, keepdims=True))
        normed = (stream_f * lax.rsqrt(mean_sq + norm_eps) * norm_weight[None, :]).astype(jnp.bfloat16)
        query_key = jnp.dot(normed, query_key_weight, preferred_element_type=jnp.float32).astype(jnp.bfloat16)
        plain_value_rows = jnp.dot(normed, value_weight, preferred_element_type=jnp.float32)
        token_adapter = jnp.repeat(adapters, BLK)
        low_all = lax.dot_general(normed, flattened_down, (((1,), (1,)), ((), ())), preferred_element_type=jnp.float32)
        reduced_rows = jnp.where(token_adapter[:, None] == owner[None, :], low_all, 0.0).astype(jnp.bfloat16)
        adapter_delta = (adapter_scale * jnp.dot(reduced_rows, flattened_up, preferred_element_type=jnp.float32)).astype(jnp.bfloat16)
        value_matrix = plain_value_rows + adapter_delta.astype(jnp.float32)
        segment = prompt_index(lengths, TOK_DEV)
        conv = short_conv(value_matrix, convolution_weights, segment)
        mixed = (conv * jax.nn.silu(value_matrix)).astype(jnp.bfloat16)
        attended = taylor_heads(query_key, mixed, segment, HEADS, QK)
        return (stream_f + jnp.dot(attended, output_weight, preferred_element_type=jnp.float32)).astype(jnp.bfloat16)
    blocks = (stream.reshape(DEVICES, TOK_DEV, MODEL_WIDTH), prompt_lengths, block_adapter_index.reshape(DEVICES, TOK_DEV // BLK))
    return lax.map(device_layer, blocks).reshape(TOKENS, MODEL_WIDTH)
```

```python
import functools
import math

import jax
import jax.numpy as jnp
from jax import lax
from jax.experimental import pallas as pl
from jax.experimental.pallas import tpu as pltpu
from jax.sharding import PartitionSpec as P

HEADS = 16
QK = 16
BAND = 256
STRIP = 128
AXES = ("dp", "mp")

adapter_scale = 2.0
norm_eps = 1e-05

VMEM_LIMIT = 56 * 1024 * 1024


def params(dims):
    return pltpu.CompilerParams(
        dimension_semantics=("arbitrary",) * dims, vmem_limit_bytes=VMEM_LIMIT
    )


def cost(flops, moved):
    return pl.CostEstimate(flops=int(flops), bytes_accessed=int(moved), transcendentals=0)


def dot(a, b):
    return jnp.dot(a, b, preferred_element_type=jnp.float32)


def whole(shape):
    return pl.BlockSpec(shape, lambda *_: (0,) * len(shape))


def smem():
    return pl.BlockSpec(memory_space=pltpu.SMEM)


def split_features(source, own, far, order, blocks, rows):
    width = source.shape[1] // blocks
    half = width // 2
    core = order[blocks]
    for pair in range(blocks // 2):
        first = source[rows, pl.ds(pl.multiple_of(order[2 * pair] * width, width), width)]
        second = source[rows, pl.ds(pl.multiple_of(order[2 * pair + 1] * width, width), width)]
        low = jnp.concatenate([first[:, :half], second[:, :half]], axis=1)
        high = jnp.concatenate([first[:, half:], second[:, half:]], axis=1)
        place = slice(pair * width, (pair + 1) * width)

        @pl.when(core == 0)
        def _():
            own[rows, place] = low
            far[rows, place] = high

        @pl.when(core != 0)
        def _():
            own[rows, place] = high
            far[rows, place] = low


def norm_kernel(order, stream, gain, normed, own, far, *, blocks):
    x = stream[...].astype(jnp.float32)
    mean_sq = jnp.mean(x * x, axis=1, keepdims=True)
    normed[...] = (x * lax.rsqrt(mean_sq + norm_eps) * gain[...]).astype(jnp.bfloat16)
    split_features(normed, own, far, order, blocks, slice(None))


def norm(stream, gain, order, blocks):
    tokens, width = stream.shape
    rows = tokens // 4
    half = width // 2
    return pl.pallas_call(
        functools.partial(norm_kernel, blocks=blocks),
        grid=(4,),
        in_specs=[
            smem(),
            pl.BlockSpec((rows, width), lambda i: (i, 0)),
            whole((1, width)),
        ],
        out_specs=[
            pl.BlockSpec((rows, width), lambda i: (i, 0)),
            pl.BlockSpec((rows, half), lambda i: (i, 0)),
            pl.BlockSpec((rows, half), lambda i: (i, 0)),
        ],
        out_shape=[
            jax.ShapeDtypeStruct((tokens, width), jnp.bfloat16),
            jax.ShapeDtypeStruct((tokens, half), jnp.bfloat16),
            jax.ShapeDtypeStruct((tokens, half), jnp.bfloat16),
        ],
        compiler_params=params(1),
        cost_estimate=cost(8 * tokens * width, 6 * tokens * width),
        name="norm",
    )(order, stream, gain.reshape(1, width))


def low_kernel(adapters, normed, own, far, owner, low):
    block_count = adapters.shape[0]
    rows = normed.shape[0] // block_count
    maps = own.shape[0]
    contract = (((1,), (1,)), ((), ()))
    for place, down in ((0, own), (maps, far)):
        part = lax.dot_general(normed[...], down[...], contract, preferred_element_type=jnp.float32)
        ids = owner[:, place : place + maps]
        for block in range(block_count):
            at = slice(block * rows, (block + 1) * rows)
            kept = jnp.where(ids == adapters[block], part[at], 0.0)
            low[at, place : place + maps] = kept.astype(jnp.bfloat16)


def low_rank(adapters, normed, own, far, owner):
    tokens, width = normed.shape
    maps = own.shape[0] // 2
    return pl.pallas_call(
        low_kernel,
        grid=(1,),
        in_specs=[
            smem(),
            whole((tokens, width)),
            whole((maps, width)),
            whole((maps, width)),
            whole((1, 2 * maps)),
        ],
        out_specs=whole((tokens, 2 * maps)),
        out_shape=jax.ShapeDtypeStruct((tokens, 2 * maps), jnp.bfloat16),
        compiler_params=params(1),
        cost_estimate=cost(4 * tokens * width * maps, 2 * width * (tokens + 2 * maps)),
        name="low_rank",
    )(adapters, normed, own, far, owner)


def prompt_start(lengths, token):
    start = jnp.zeros_like(token)
    bound = 0
    for prompt in range(lengths.shape[1] - 1):
        bound = bound + lengths[0, prompt]
        start = jnp.where(token >= bound, bound, start)
    return start


def mixer_kernel(
    lengths,
    order,
    x_own,
    x_far,
    own_one,
    far_one,
    own_two,
    far_two,
    own_q,
    far_q,
    own_k,
    far_k,
    low,
    up_own,
    up_far,
    taps,
    att_own,
    att_far,
    queries,
    keys,
    values,
    reach,
    allowed,
    attended,
    *,
    blocks,
):
    step = pl.program_id(0)
    steps = pl.num_programs(0)
    tokens = x_own.shape[0]
    columns = own_one.shape[1]
    head_width = columns // 2
    strips = tokens // STRIP
    span = min(BAND // STRIP + 1, strips) * STRIP

    @pl.when(step == 0)
    def _():
        queries[...] = (dot(x_own[...], own_q[...]) + dot(x_far[...], far_q[...])).astype(
            jnp.bfloat16
        )
        keys[...] = (dot(x_own[...], own_k[...]) + dot(x_far[...], far_k[...])).astype(jnp.bfloat16)
        token = lax.broadcasted_iota(jnp.int32, (tokens, columns), 0)
        since = token - prompt_start(lengths, token)
        for offset in range(1, taps.shape[0]):
            reach[offset - 1] = (since >= offset).astype(jnp.float32)
        for strip in range(strips):
            base = max(0, (strip + 1) * STRIP - span)
            row = strip * STRIP + lax.broadcasted_iota(jnp.int32, (STRIP, span), 0)
            column = base + lax.broadcasted_iota(jnp.int32, (STRIP, span), 1)
            inside = (column <= row) & (column >= prompt_start(lengths, row))
            allowed[strip] = inside.astype(jnp.float32)

    @pl.when(step < steps // 2)
    def _():
        values[...] = dot(x_own[...], own_one[...]) + dot(x_far[...], far_one[...])

    @pl.when(step >= steps // 2)
    def _():
        values[...] = dot(x_own[...], own_two[...]) + dot(x_far[...], far_two[...])

    maps = up_own.shape[0]
    delta = dot(low[:, :maps], up_own[...]) + dot(low[:, maps:], up_far[...])
    v = values[...] + (adapter_scale * delta).astype(jnp.bfloat16).astype(jnp.float32)
    conv = taps[0:1] * v
    for offset in range(1, taps.shape[0]):
        conv = conv + taps[offset : offset + 1] * (reach[offset - 1] * pltpu.roll(v, offset, 0))
    mixed = (conv * (v / (1.0 + jnp.exp(-v)))).astype(jnp.bfloat16)

    lane = lax.broadcasted_iota(jnp.int32, (tokens, queries.shape[1]), 1) // QK
    ones = jnp.ones((span, head_width), jnp.bfloat16)
    fold = 1.0 / math.sqrt(2.0)
    scale = fold / math.sqrt(QK)
    for part in range(2):
        query = jnp.where(lane == 2 * step + part, queries[...], jnp.zeros((), jnp.bfloat16))
        mine = mixed[:, part * head_width : (part + 1) * head_width]
        for strip in range(strips):
            rows = slice(strip * STRIP, (strip + 1) * STRIP)
            end = (strip + 1) * STRIP
            base = max(0, end - span)
            near = slice(base, end)
            score = lax.dot_general(
                query[rows],
                keys[near, :],
                (((1,), (1,)), ((), ())),
                preferred_element_type=jnp.float32,
            )
            shifted = score * scale + fold
            weight = (shifted * shifted + 0.5) * allowed[strip, :, : end - base]
            both = jnp.concatenate([mine[near], ones[: end - base]], axis=1)
            total = dot(weight.astype(jnp.bfloat16), both)
            result = total[:, :head_width] / total[:, head_width:]
            place = pl.multiple_of((2 * step + part) * head_width, head_width)
            attended[rows, pl.ds(place, head_width)] = result.astype(jnp.bfloat16)

    @pl.when(step == steps - 1)
    def _():
        for strip in range(strips):
            rows = slice(strip * STRIP, (strip + 1) * STRIP)
            split_features(attended, att_own, att_far, order, blocks, rows)


def mixer(lengths, order, x_own, x_far, one, two, adapters, low, taps, blocks):
    tokens, half = x_own.shape
    width = taps.shape[1]
    columns = 2 * (width // HEADS)
    steps = HEADS // 2
    features = HEADS * QK
    qk_block = (width // 2) // features
    maps = adapters[0].shape[0] // 2
    strips = tokens // STRIP
    span = min(BAND // STRIP + 1, strips) * STRIP
    first = pl.BlockSpec((half, columns), lambda i: (0, jnp.minimum(i, steps // 2 - 1)))
    second = pl.BlockSpec((half, columns), lambda i: (0, jnp.maximum(i - steps // 2, 0)))
    side = pl.BlockSpec((half, features), lambda i: (0, qk_block))
    up = pl.BlockSpec((maps, columns), lambda i: (1, i))
    flops = 2 * tokens * width * (width + 2 * features + 2 * maps)
    return pl.pallas_call(
        functools.partial(mixer_kernel, blocks=blocks),
        grid=(steps,),
        in_specs=[
            smem(),
            smem(),
            whole((tokens, half)),
            whole((tokens, half)),
            first,
            first,
            second,
            second,
            side,
            side,
            side,
            side,
            whole((tokens, 2 * maps)),
            up,
            up,
            pl.BlockSpec((taps.shape[0], columns), lambda i: (0, i)),
        ],
        out_specs=[whole((tokens, half))] * 2,
        out_shape=[jax.ShapeDtypeStruct((tokens, half), jnp.bfloat16)] * 2,
        scratch_shapes=[
            pltpu.VMEM((tokens, features), jnp.bfloat16),
            pltpu.VMEM((tokens, features), jnp.bfloat16),
            pltpu.VMEM((tokens, columns), jnp.float32),
            pltpu.VMEM((taps.shape[0] - 1, tokens, columns), jnp.float32),
            pltpu.VMEM((strips, STRIP, span), jnp.float32),
            pltpu.VMEM((tokens, width), jnp.bfloat16),
        ],
        compiler_params=params(1),
        cost_estimate=cost(2 * flops, 2 * width * (width + 2 * features) + 8 * tokens * width),
        name="mixer",
    )(
        lengths,
        order,
        x_own,
        x_far,
        one[0],
        one[1],
        two[0],
        two[1],
        one[0],
        one[1],
        two[0],
        two[1],
        low,
        adapters[0],
        adapters[1],
        taps,
    )


def project_kernel(base, att_own, att_far, own, far, out):
    total = base[...].astype(jnp.float32) + (
        dot(att_own[...], own[...]) + dot(att_far[...], far[...])
    )
    out[...] = total.astype(out.dtype)


def project(base, att_own, att_far, own, far, place, dtype):
    tokens, width = base.shape
    rows = own.shape[0]
    columns = 512
    column_block = pl.BlockSpec((tokens, columns), lambda j: (0, j))
    feature_block = pl.BlockSpec((tokens, rows), lambda j: (0, place))
    weight_block = pl.BlockSpec((rows, columns), lambda j: (0, j))
    return pl.pallas_call(
        project_kernel,
        grid=(width // columns,),
        in_specs=[column_block, feature_block, feature_block, weight_block, weight_block],
        out_specs=column_block,
        out_shape=jax.ShapeDtypeStruct((tokens, width), dtype),
        compiler_params=params(1),
        cost_estimate=cost(4 * tokens * width * rows, 4 * width * rows + 6 * tokens * width),
        name="project",
    )(base, att_own, att_far, own, far)


def moves():
    def perm(to):
        pairs = []
        for z in range(4):
            for y in range(2):
                for x in range(2):
                    for c in range(2):
                        there = to(z, y, x, c)
                        target = ((there[0] * 2 + there[1]) * 2 + there[2]) * 2 + there[3]
                        pairs.append((((z * 2 + y) * 2 + x) * 2 + c, target))
        return pairs

    table = {
        "x": perm(lambda z, y, x, c: (z, y, 1 - x, c)),
        "y": perm(lambda z, y, x, c: (z, 1 - y, x, c)),
        "z": perm(lambda z, y, x, c: ((z + 1) % 4, y, x, c)),
        "c": perm(lambda z, y, x, c: (z, y, x, 1 - c)),
    }
    return {name: functools.partial(lax.ppermute, axis_name=AXES, perm=p) for name, p in table.items()}


def cube_gather(shard, first, last):
    move = moves()
    ring = [jnp.concatenate([shard, move[first](shard)], axis=0)]
    for _ in range(3):
        ring.append(move["z"](ring[-1]))
    return [(block, move[last](block)) for block in ring]


def in_order(blocks, rows, swapped):
    pieces = []
    for near, next_to in blocks:
        if swapped:
            pieces += [near[:rows], next_to[:rows], near[rows:], next_to[rows:]]
        else:
            pieces += [near, next_to]
    return jnp.concatenate(pieces, axis=0)


def cube_local(
    stream,
    norm_weight,
    query_key_weight,
    value_weight,
    output_weight,
    convolution_weights,
    adapter_down_maps,
    adapter_up_maps,
    prompt_lengths,
    block_adapter_index,
):
    move = moves()
    width = stream.shape[1]
    half = width // 2
    features = query_key_weight.shape[1] // 2
    rows = value_weight.shape[0]
    held, rank = adapter_down_maps.shape[:2]
    z = lax.axis_index("dp")
    mp = lax.axis_index("mp")
    y, x, core = mp // 4, (mp // 2) % 2, mp % 2

    step = jnp.arange(16, dtype=jnp.int32)
    chips = ((z - step // 4) % 4) * 4 + (y ^ ((step // 2) % 2)) * 2 + (x ^ (step % 2))
    order = jnp.concatenate([chips, core[None]]).astype(jnp.int32)
    normed, x_own, x_far = norm(stream, norm_weight, order, 16)

    own = jnp.concatenate(
        [adapter_down_maps.reshape(held * rank, width), adapter_up_maps.reshape(held * rank, width)],
        axis=0,
    )
    maps = held * rank
    from_x, from_y = move["x"](own), move["y"](own)
    cross_down, cross_up = move["x"](from_y[:maps]), move["y"](from_x[maps:])
    adapters_own = jnp.concatenate(
        [own[:maps], from_x[:maps], from_y[:maps], cross_down]
        + [own[maps:], from_x[maps:], from_y[maps:], cross_up],
        axis=0,
    )
    adapters = (adapters_own, move["c"](adapters_own))
    slot = jnp.arange(8, dtype=jnp.int32)
    holder = (y ^ ((slot // 2) % 2)) * 4 + (x ^ (slot % 2)) * 2 + (core ^ (slot // 4))
    owner = (holder[:, None] * held + jnp.arange(maps, dtype=jnp.int32)[None, :] // rank).reshape(1, -1)
    low = low_rank(block_adapter_index, normed, adapters[0], adapters[1], owner)

    one = jnp.concatenate([value_weight[:, :half], query_key_weight[:, :features]], axis=1)
    two = jnp.concatenate([value_weight[:, half:], query_key_weight[:, features:]], axis=1)
    one = in_order(cube_gather(one, "x", "y"), rows, False)
    two = in_order(cube_gather(two, "y", "x"), rows, True)
    one, two = (one, move["c"](one)), (two, move["c"](two))
    att_own, att_far = mixer(
        prompt_lengths, order, x_own, x_far, one, two, adapters, low, convolution_weights, 16
    )

    left = cube_gather(output_weight[:, :half], "x", "y")
    right = cube_gather(output_weight[:, half:], "y", "x")
    early = jnp.concatenate([in_order(left[:3], rows, False), in_order(right[:3], rows, True)], axis=1)
    late = jnp.concatenate([in_order(left[3:], rows, False), in_order(right[3:], rows, True)], axis=1)
    total = project(stream, att_own, att_far, early, move["c"](early), 0, jnp.float32)
    return project(total, att_own, att_far, late, move["c"](late), 3, jnp.bfloat16)


def plain_local(
    stream,
    norm_weight,
    query_key_weight,
    value_weight,
    output_weight,
    convolution_weights,
    adapter_down_maps,
    adapter_up_maps,
    prompt_lengths,
    block_adapter_index,
):
    width = stream.shape[1]
    half = width // 2
    features = query_key_weight.shape[1] // 2
    gather = functools.partial(lax.all_gather, axis_name=AXES, axis=0, tiled=True)
    order = jnp.arange(17, dtype=jnp.int32) % 16
    normed, x_own, x_far = norm(stream, norm_weight, order, 16)
    blocked = lambda w: w.reshape(16, 2, width // 32, w.shape[1])
    halves = lambda w: (blocked(w)[:, 0].reshape(half, -1), blocked(w)[:, 1].reshape(half, -1))
    down = lax.all_gather(adapter_down_maps, "mp", axis=0, tiled=True)
    up = lax.all_gather(adapter_up_maps, "mp", axis=0, tiled=True)
    count, rank = down.shape[:2]
    maps = count * rank // 2
    down, up = down.reshape(2 * maps, width), up.reshape(2 * maps, width)
    adapters = tuple(
        jnp.concatenate([down[at : at + maps], up[at : at + maps]], axis=0) for at in (0, maps)
    )
    owner = (jnp.arange(2 * maps, dtype=jnp.int32) // rank).reshape(1, -1)
    low = low_rank(block_adapter_index, normed, adapters[0], adapters[1], owner)
    value_rows, qk_rows = gather(value_weight), gather(query_key_weight)
    one = jnp.concatenate([value_rows[:, :half], qk_rows[:, :features]], axis=1)
    two = jnp.concatenate([value_rows[:, half:], qk_rows[:, features:]], axis=1)
    att_own, att_far = mixer(
        prompt_lengths,
        order,
        x_own,
        x_far,
        halves(one),
        halves(two),
        adapters,
        low,
        convolution_weights,
        16,
    )
    out_own, out_far = halves(gather(output_weight))
    return project(stream, att_own, att_far, out_own, out_far, 0, jnp.bfloat16)


def solution(mesh):
    cube = dict(mesh.shape) == {"dp": 4, "mp": 8}
    return jax.shard_map(
        cube_local if cube else plain_local,
        mesh=mesh,
        in_specs=(
            P(AXES, None),
            P(),
            P(AXES, None),
            P(AXES, None),
            P(AXES, None),
            P(),
            P("mp", None, None),
            P("mp", None, None),
            P(AXES, None),
            P(AXES),
        ),
        out_specs=P(AXES, None),
        check_vma=False,
    )
```

```python
import functools
import math

import jax
import jax.numpy as jnp
from jax import lax
from jax.experimental import pallas as pl
from jax.experimental.pallas import tpu as pltpu
from jax.sharding import PartitionSpec as P

HEADS = 16
QK = 16
BAND = 256
STRIP = 256
ROWS = 128
AXES = ("dp", "mp")

adapter_scale = 2.0
norm_eps = 1e-05

MIB = 1024 * 1024
VMEM = pl.BlockSpec(memory_space=pltpu.VMEM)
SMEM = pl.BlockSpec(memory_space=pltpu.SMEM)
ANY = pl.BlockSpec(memory_space=pl.ANY)


def params(mib):
    return pltpu.CompilerParams(vmem_limit_bytes=mib * MIB)


def cost(micros):
    return pl.CostEstimate(flops=int(micros * 1.1e9), bytes_accessed=0, transcendentals=0)


def dot(a, b):
    return jnp.dot(a, b, preferred_element_type=jnp.float32)


def dot_t(a, b):
    return lax.dot_general(a, b, (((1,), (1,)), ((), ())), preferred_element_type=jnp.float32)


class Rows:
    def __init__(self, pieces):
        self.arrays = []
        self.pieces = []
        for array, first, rows in pieces:
            known = [i for i, other in enumerate(self.arrays) if other is array]
            if not known:
                self.arrays.append(array)
                known = [len(self.arrays) - 1]
            self.pieces.append((known[0], first, rows))
        self.rows = sum(rows for _, _, rows in self.pieces)

    def take(self, refs, columns):
        parts = [refs[i][first : first + rows, columns] for i, first, rows in self.pieces]
        return parts[0] if len(parts) == 1 else jnp.concatenate(parts, axis=0)


class Layout:
    blocks = 16

    def place(self, block):
        return block

    def swap(self, value):
        return value

    def owner(self, count, rank):
        return lax.broadcasted_iota(jnp.int32, (1, count), 1) // rank


class CubeLayout(Layout):
    def __init__(self, held):
        self.held = held

    def position(self):
        mp = lax.axis_index("mp")
        return lax.axis_index("dp"), mp // 4, (mp // 2) % 2, mp % 2

    def place(self, block):
        z, y, x, core = self.position()
        step = (z + 4 - block // 4) % 4
        off_y = lax.bitwise_xor(y, (block // 2) % 2)
        off_x = lax.bitwise_xor(x, block % 2)
        return step * 4 + off_y * (2 - core) + off_x * (1 + core)

    def swap(self, value):
        core = lax.axis_index("mp") % 2
        return jnp.where(core != 0, pltpu.roll(value, value.shape[1] // 2, 1), value)

    def owner(self, count, rank):
        _, y, x, core = self.position()
        column = lax.broadcasted_iota(jnp.int32, (1, count), 1)
        maps = self.held * rank
        slot = column // maps
        its_core = lax.bitwise_xor(core, slot // 4)
        to_first, to_last = slot % 2, (slot // 2) % 2
        its_y = lax.bitwise_xor(y, jnp.where(its_core == 0, to_last, to_first))
        its_x = lax.bitwise_xor(x, jnp.where(its_core == 0, to_first, to_last))
        return (its_y * 4 + its_x * 2 + its_core) * self.held + (column % maps) // rank


def put_block(target, rows, block, layout, value):
    width = target.shape[1] // layout.blocks
    at = pl.multiple_of(layout.place(block) * width, width)
    target[rows, pl.ds(at, width)] = layout.swap(value).astype(jnp.bfloat16)


def norm_kernel(stream, gain, normed, ordered, *, layout):
    tokens, width = stream.shape
    blocks = layout.blocks
    block_width = width // blocks

    @pl.loop(0, tokens // ROWS)
    def _(i):
        rows = pl.ds(pl.multiple_of(i * ROWS, ROWS), ROWS)
        x = stream[rows].astype(jnp.float32)
        mean_sq = jnp.mean(x * x, axis=1, keepdims=True)
        y = x * lax.rsqrt(mean_sq + norm_eps) * gain[...]
        normed[rows] = y.astype(jnp.bfloat16)
        for block in range(blocks):
            part = y[:, block * block_width : (block + 1) * block_width]
            put_block(ordered, rows, block, layout, part)


def norm(stream, gain, layout):
    tokens, width = stream.shape
    return pl.pallas_call(
        functools.partial(norm_kernel, layout=layout),
        in_specs=[VMEM, VMEM],
        out_specs=[VMEM, VMEM],
        out_shape=[jax.ShapeDtypeStruct((tokens, width), jnp.bfloat16)] * 2,
        compiler_params=params(10),
        cost_estimate=cost(2.5),
        name="norm",
    )(stream, gain.reshape(1, width))


def low_kernel(adapters, normed, *rest, down, layout, rank):
    refs, low = rest[:-1], rest[-1]
    block_count = adapters.shape[0]
    rows = normed.shape[0] // block_count
    owner = layout.owner(down.rows, rank)
    all_low = dot_t(normed[...], down.take(refs, slice(None)))
    for block in range(block_count):
        at = slice(block * rows, (block + 1) * rows)
        low[at] = jnp.where(owner == adapters[block], all_low[at], 0.0).astype(jnp.bfloat16)


def low_rank(adapters, normed, down, layout, rank):
    tokens, width = normed.shape
    return pl.pallas_call(
        functools.partial(low_kernel, down=down, layout=layout, rank=rank),
        in_specs=[SMEM, VMEM] + [VMEM] * len(down.arrays),
        out_specs=VMEM,
        out_shape=jax.ShapeDtypeStruct((tokens, down.rows), jnp.bfloat16),
        compiler_params=params(10),
        cost_estimate=cost(2.0),
        name="low_rank",
    )(adapters, normed, *down.arrays)


def prompt_start(lengths, token):
    start = jnp.zeros_like(token)
    bound = 0
    for prompt in range(lengths.shape[1] - 1):
        bound = bound + lengths[0, prompt]
        start = jnp.where(token >= bound, bound, start)
    return start


def prompts_kernel(lengths, reach, allowed):
    tokens, head_width = reach.shape[1:]
    token = lax.broadcasted_iota(jnp.int32, (tokens, head_width), 0)
    since = token - prompt_start(lengths, token)
    for offset in range(1, reach.shape[0] + 1):
        reach[offset - 1] = (since >= offset).astype(jnp.float32)
    for strip, span in enumerate(spans(tokens)):
        row = strip * STRIP + lax.broadcasted_iota(jnp.int32, (STRIP, span), 0)
        column = (strip + 1) * STRIP - span + lax.broadcasted_iota(jnp.int32, (STRIP, span), 1)
        inside = (column <= row) & (column >= prompt_start(lengths, row))
        allowed[strip, :, :span] = inside.astype(jnp.bfloat16)


def spans(tokens):
    return [min((i + 1) * STRIP, STRIP + BAND) for i in range(tokens // STRIP)]


def prompts(lengths, tokens, head_width, taps):
    return pl.pallas_call(
        prompts_kernel,
        in_specs=[SMEM],
        out_specs=[VMEM, VMEM],
        out_shape=[
            jax.ShapeDtypeStruct((taps - 1, tokens, head_width), jnp.float32),
            jax.ShapeDtypeStruct((tokens // STRIP, STRIP, STRIP + BAND), jnp.bfloat16),
        ],
        compiler_params=params(8),
        cost_estimate=cost(1.0),
        name="prompts",
    )(lengths)


def query_key_kernel(ordered, *rest, weights, first):
    refs, out = rest[:-1], rest[-1]
    columns = out.shape[1]
    out[...] = dot(ordered[...], weights.take(refs, slice(first, first + columns))).astype(jnp.bfloat16)


def query_key(ordered, weights, first, columns):
    tokens, width = ordered.shape
    return pl.pallas_call(
        functools.partial(query_key_kernel, weights=weights, first=first),
        in_specs=[VMEM] * (1 + len(weights.arrays)),
        out_specs=VMEM,
        out_shape=jax.ShapeDtypeStruct((tokens, columns), jnp.bfloat16),
        compiler_params=params(10),
        cost_estimate=cost(2.7),
        name="query_key",
    )(ordered, *weights.arrays)


def mixer_kernel(
    ordered, qk, low, taps, reach, allowed, *rest, weights, up, layout, group, first, heads
):
    refs = rest[: len(weights.arrays)]
    refs_up = rest[len(weights.arrays) : len(weights.arrays) + len(up.arrays)]
    attended = rest[-1]
    tokens, width = ordered.shape
    head_width = width // HEADS
    columns = group * head_width
    features = HEADS * QK
    lane = lax.broadcasted_iota(jnp.int32, (tokens, features), 1) // QK
    ones = jnp.ones((max(spans(tokens)), head_width), jnp.bfloat16)
    for begin in range(first, first + heads, group):
        here = slice(begin * head_width, begin * head_width + columns)
        v = dot(ordered[...], weights.take(refs, here))
        delta = adapter_scale * dot(low[...], up.take(refs_up, here))
        v = v + delta.astype(jnp.bfloat16).astype(jnp.float32)
        tap = taps[:, here]
        conv = tap[0:1] * v
        for offset in range(1, taps.shape[0]):
            seen = jnp.concatenate([reach[offset - 1]] * group, axis=1)
            conv = conv + tap[offset : offset + 1] * (seen * pltpu.roll(v, offset, 0))
        mixed = (conv * (0.5 * v + 0.5 * v * jnp.tanh(0.5 * v))).astype(jnp.bfloat16)
        for part in range(group):
            head = begin + part
            query = jnp.where(lane == head, qk[:, :features], jnp.zeros((), jnp.bfloat16))
            mine = mixed[:, part * head_width : (part + 1) * head_width]
            for strip, span in enumerate(spans(tokens)):
                end = (strip + 1) * STRIP
                rows = slice(end - STRIP, end)
                near = slice(end - span, end)
                score = dot_t(query[rows], qk[near, features:]) + float(QK) ** 0.5
                weight = (score * score + float(QK)).astype(jnp.bfloat16)
                weight = weight * allowed[strip, :, :span]
                both = jnp.concatenate([mine[near], ones[:span]], axis=1)
                total = dot(weight, both)
                result = total[:, :head_width] / total[:, head_width:]
                put_block(attended, rows, head, layout, result)


def mixer(ordered, qk, low, taps, masks, weights, up, layout, first, heads, attended):
    tokens, width = ordered.shape
    fresh = attended is None
    inputs = [ordered, qk, low, taps, *masks, *weights.arrays, *up.arrays]
    if not fresh:
        inputs.append(attended)
    return pl.pallas_call(
        functools.partial(
            mixer_kernel,
            weights=weights,
            up=up,
            layout=layout,
            group=min(heads, 4),
            first=first,
            heads=heads,
        ),
        in_specs=[VMEM] * len(inputs),
        out_specs=VMEM,
        out_shape=jax.ShapeDtypeStruct((tokens, width), jnp.bfloat16),
        input_output_aliases={} if fresh else {len(inputs) - 1: 0},
        compiler_params=params(10),
        cost_estimate=cost(1.2 * heads),
        name="mixer",
    )(*inputs)


def project_kernel(base, attended, *rest, sides, quarters, columns, last):
    tokens, width = base.shape
    side_width = width // len(sides)
    count = sum(len(side.arrays) for side in sides)
    refs, out, scratch = rest[:count], rest[count], rest[count + 1 :]
    quarter = width // 4
    x = [attended[:, q * quarter : (q + 1) * quarter] for q in quarters]
    x = x[0] if len(x) == 1 else jnp.concatenate(x, axis=1)
    copies = []
    at = 0
    for number, side in enumerate(sides):
        own = refs[at : at + len(side.arrays)]
        at += len(side.arrays)
        for begin in range(0, side_width, columns):
            place = slice(number * side_width + begin, number * side_width + begin + columns)
            total = base[:, place].astype(jnp.float32)
            total = total + dot(x, side.take(own, slice(begin, begin + columns)))
            if last:
                stage, arrived = scratch
                slot = len(copies)
                stage[slot] = total.astype(jnp.bfloat16)
                copies.append(pltpu.make_async_copy(stage.at[slot], out.at[:, place], arrived.at[slot]))
                copies[-1].start()
            else:
                out[:, place] = total
    for copy in copies:
        copy.wait()


def project(base, attended, sides, quarters, last):
    tokens, width = base.shape
    columns = 512
    slots = width // columns
    arrays = [array for side in sides for array in side.arrays]
    scratch = [pltpu.VMEM((slots, tokens, columns), jnp.bfloat16), pltpu.SemaphoreType.DMA((slots,))]
    return pl.pallas_call(
        functools.partial(project_kernel, sides=sides, quarters=quarters, columns=columns, last=last),
        in_specs=[VMEM, VMEM] + [VMEM] * len(arrays),
        out_specs=ANY if last else VMEM,
        out_shape=jax.ShapeDtypeStruct((tokens, width), jnp.bfloat16 if last else jnp.float32),
        scratch_shapes=scratch if last else [],
        compiler_params=params(10),
        cost_estimate=cost(1.0 + 1.2 * len(quarters)),
        name="project",
    )(base, attended, *arrays)


def moves():
    def perm(to):
        pairs = []
        for z in range(4):
            for y in range(2):
                for x in range(2):
                    for c in range(2):
                        there = to(z, y, x, c)
                        target = ((there[0] * 2 + there[1]) * 2 + there[2]) * 2 + there[3]
                        pairs.append((((z * 2 + y) * 2 + x) * 2 + c, target))
        return pairs

    table = {
        "first": perm(lambda z, y, x, c: (z, y ^ c, x ^ (1 - c), c)),
        "last": perm(lambda z, y, x, c: (z, y ^ (1 - c), x ^ c, c)),
        "up": perm(lambda z, y, x, c: ((z + 1) % 4, y, x, c)),
        "down": perm(lambda z, y, x, c: ((z + 3) % 4, y, x, c)),
        "core": perm(lambda z, y, x, c: (z, y, x, 1 - c)),
    }
    return {name: functools.partial(lax.ppermute, axis_name=AXES, perm=p) for name, p in table.items()}


def after(value, *others):
    return lax.optimization_barrier((value, *others))[0]


def join(*parts):
    return jnp.concatenate(parts, axis=0)


def both_cores(steps, rows):
    swap = moves()["core"]
    swapped = {}
    for step in steps:
        for array, _ in step:
            if id(array) not in swapped:
                swapped[id(array)] = swap(array)
    pieces = []
    for here, to_first, to_last, across in steps:
        for (own, at), (far, far_at) in (
            (here, here),
            (to_first, to_last),
            (to_last, to_first),
            (across, across),
        ):
            pieces += [(own, at, rows), (swapped[id(far)], far_at, rows)]
    return Rows(pieces)


def cube_local(
    stream,
    norm_weight,
    query_key_weight,
    value_weight,
    output_weight,
    convolution_weights,
    adapter_down_maps,
    adapter_up_maps,
    prompt_lengths,
    block_adapter_index,
):
    move = moves()
    first, last, above, below, swap = (move[n] for n in ("first", "last", "up", "down", "core"))
    tokens, width = stream.shape
    rows = value_weight.shape[0]
    held, rank = adapter_down_maps.shape[:2]
    maps = held * rank
    layout = CubeLayout(held)

    a = jnp.concatenate([value_weight, query_key_weight], axis=1)
    d = jnp.concatenate(
        [adapter_down_maps.reshape(maps, width), adapter_up_maps.reshape(maps, width)], axis=0
    )
    a1, a3 = above(a), below(a)
    fa, la = first(a), last(a)
    xa = last(fa)
    fd, ld = first(d), last(d)
    xd = last(fd)
    e = output_weight
    normed, ordered = norm(stream, norm_weight, layout)
    masks = prompts(prompt_lengths, tokens, width // HEADS, convolution_weights.shape[0])
    fe = first(after(e, fa))
    a2 = above(a1)
    b = join(after(a1, fa, la, fe, ordered, masks[0]), a3)
    fb, lb = first(b), last(b)
    xb = last(fb)
    f2, l2 = first(a2), last(a2)
    o0 = after(join(e, fe), a2)
    o1, o3 = above(o0), below(o0)
    x2 = last(after(f2, o1, o3))
    o2 = above(after(o1, f2, l2, xd))
    values = both_cores(
        [
            tuple((p, 0) for p in (a, fa, la, xa)),
            tuple((p, 0) for p in (b, fb, lb, xb)),
            tuple((p, 0) for p in (a2, f2, l2, x2)),
            tuple((p, rows) for p in (b, fb, lb, xb)),
        ],
        rows,
    )
    near = (d, fd, ld, xd)
    far = [swap(p) for p in near]
    down = Rows([(p, 0, maps) for p in (*near, *far)])
    up = Rows([(p, maps, maps) for p in (*near, *far)])
    low = low_rank(block_adapter_index, normed, down, layout, rank)

    rest = [last(p) for p in (o0, o1, o2, o3)]
    qk = query_key(after(ordered, o2), values, width, 2 * HEADS * QK)
    attended = None
    heads = HEADS // 4
    for part in range(4):
        attended = mixer(
            ordered, qk, low, convolution_weights, masks, values, up, layout, part * heads, heads, attended
        )
    pieces = [((p, 0), (p, rows), (q, 0), (q, rows)) for p, q in zip((o0, o1, o2, o3), rest)]
    early = both_cores([pieces[0], pieces[1], pieces[3]], rows)
    late = both_cores([pieces[2]], rows)
    order = (0, 1, 3)
    total = project(stream, attended, [early], order, False)
    return project(total, attended, [late], (2,), True)


def plain_local(
    stream,
    norm_weight,
    query_key_weight,
    value_weight,
    output_weight,
    convolution_weights,
    adapter_down_maps,
    adapter_up_maps,
    prompt_lengths,
    block_adapter_index,
):
    width = stream.shape[1]
    gather = functools.partial(lax.all_gather, axis_name=AXES, axis=0, tiled=True)
    layout = Layout()
    normed, ordered = norm(stream, norm_weight, layout)
    down = lax.all_gather(adapter_down_maps, "mp", axis=0, tiled=True)
    up = lax.all_gather(adapter_up_maps, "mp", axis=0, tiled=True)
    count, rank = down.shape[:2]
    maps = count * rank
    everything = lambda w: Rows([(w, 0, w.shape[0])])
    low = low_rank(block_adapter_index, normed, everything(down.reshape(maps, width)), layout, rank)
    values = everything(jnp.concatenate([gather(value_weight), gather(query_key_weight)], axis=1))
    qk = query_key(ordered, values, width, 2 * HEADS * QK)
    masks = prompts(prompt_lengths, stream.shape[0], width // HEADS, convolution_weights.shape[0])
    up = everything(up.reshape(maps, width))
    attended = mixer(
        ordered, qk, low, convolution_weights, masks, values, up, layout, 0, HEADS, None
    )
    return project(stream, attended, [everything(gather(output_weight))], (0, 1, 2, 3), True)


def solution(mesh):
    cube = dict(mesh.shape) == {"dp": 4, "mp": 8}
    return jax.shard_map(
        cube_local if cube else plain_local,
        mesh=mesh,
        in_specs=(
            P(AXES, None),
            P(),
            P(AXES, None),
            P(AXES, None),
            P(AXES, None),
            P(),
            P("mp", None, None),
            P("mp", None, None),
            P(AXES, None),
            P(AXES),
        ),
        out_specs=P(AXES, None),
        check_vma=False,
    )
```

```python
import functools
import math

import jax
import jax.numpy as jnp
from jax import lax
from jax.experimental import pallas as pl
from jax.experimental.pallas import tpu as pltpu
from jax.sharding import PartitionSpec as P

HEADS = 16
QK = 16
BAND = 256
STRIP = 256
ROWS = 128
AXES = ("dp", "mp")

adapter_scale = 2.0
norm_eps = 1e-05

MIB = 1024 * 1024
VMEM = pl.BlockSpec(memory_space=pltpu.VMEM)
SMEM = pl.BlockSpec(memory_space=pltpu.SMEM)
ANY = pl.BlockSpec(memory_space=pl.ANY)


def params(mib):
    return pltpu.CompilerParams(vmem_limit_bytes=mib * MIB)


def cost(micros):
    return pl.CostEstimate(flops=int(micros * 1.1e9), bytes_accessed=0, transcendentals=0)


def dot(a, b):
    return jnp.dot(a, b, preferred_element_type=jnp.float32)


def dot_t(a, b):
    return lax.dot_general(a, b, (((1,), (1,)), ((), ())), preferred_element_type=jnp.float32)


class Rows:
    def __init__(self, pieces):
        self.arrays = []
        self.pieces = []
        for array, first, rows in pieces:
            known = [i for i, other in enumerate(self.arrays) if other is array]
            if not known:
                self.arrays.append(array)
                known = [len(self.arrays) - 1]
            self.pieces.append((known[0], first, rows))
        self.rows = sum(rows for _, _, rows in self.pieces)

    def take(self, refs, columns):
        parts = [refs[i][first : first + rows, columns] for i, first, rows in self.pieces]
        return parts[0] if len(parts) == 1 else jnp.concatenate(parts, axis=0)


class Layout:
    blocks = 16
    sets = 1
    heads = HEADS

    def core(self):
        return 0

    def place(self, block):
        return block

    def swap(self, value):
        return value

    def owner(self, count, rank):
        return lax.broadcasted_iota(jnp.int32, (1, count), 1) // rank


class CubeLayout(Layout):
    sets = 2
    heads = HEADS // 2

    def __init__(self, held):
        self.held = held

    def core(self):
        return lax.axis_index("mp") % 2

    def position(self):
        mp = lax.axis_index("mp")
        return lax.axis_index("dp"), mp // 4, (mp // 2) % 2, mp % 2

    def place(self, block):
        z, y, x, core = self.position()
        step = (z + 4 - block // 4) % 4
        off_y = lax.bitwise_xor(y, (block // 2) % 2)
        off_x = lax.bitwise_xor(x, block % 2)
        return step * 4 + off_y * (2 - core) + off_x * (1 + core)

    def swap(self, value):
        return jnp.where(self.core() != 0, pltpu.roll(value, value.shape[1] // 2, 1), value)

    def owner(self, count, rank):
        _, y, x, core = self.position()
        column = lax.broadcasted_iota(jnp.int32, (1, count), 1)
        maps = self.held * rank
        slot = column // maps
        to_first, to_last = slot % 2, slot // 2
        its_y = lax.bitwise_xor(y, jnp.where(core == 0, to_last, to_first))
        its_x = lax.bitwise_xor(x, jnp.where(core == 0, to_first, to_last))
        return (its_y * 4 + its_x * 2 + core) * self.held + (column % maps) // rank


def block_at(layout, block, width):
    return pl.ds(pl.multiple_of(layout.place(block) * width, width), width)


def shape(*dims, dtype=jnp.bfloat16):
    return jax.ShapeDtypeStruct(dims, dtype)


def call(kernel, outs, smem, vmem, mib, micros, name, scratch=(), out_specs=None, aliases=None):
    return pl.pallas_call(
        kernel,
        in_specs=[SMEM] * len(smem) + [VMEM] * len(vmem),
        out_specs=out_specs or jax.tree.map(lambda _: VMEM, outs),
        out_shape=outs,
        scratch_shapes=list(scratch),
        compiler_params=params(mib),
        cost_estimate=cost(micros),
        name=name,
    )(*smem, *vmem)


def norm(streams, gain, layout):
    sets = len(streams)
    tokens, width = streams[0].shape
    kept = width // sets
    block_width = width // layout.blocks

    def kernel(*refs):
        ins, weight, (normed, ordered, base) = refs[:sets], refs[sets], refs[sets + 1 :]
        core = layout.core()
        for number, source in enumerate(ins):
            at = 0 if sets == 1 else (core if number == 0 else 1 - core)

            @pl.loop(0, tokens // ROWS)
            def _(i):
                rows = pl.ds(pl.multiple_of(i * ROWS, ROWS), ROWS)
                x = source[rows].astype(jnp.float32)
                mean_sq = jnp.mean(x * x, axis=1, keepdims=True)
                y = x * lax.rsqrt(mean_sq + norm_eps) * weight[...]
                normed[at, rows] = y.astype(jnp.bfloat16)
                for block in range(layout.blocks):
                    part = y[:, block * block_width : (block + 1) * block_width]
                    place = block_at(layout, block, block_width)
                    ordered[at, rows, place] = layout.swap(part).astype(jnp.bfloat16)
                base[at, rows] = source[rows, pl.ds(pl.multiple_of(core * kept, kept), kept)]

    outs = [shape(sets, tokens, width), shape(sets, tokens, width), shape(sets, tokens, kept)]
    return call(kernel, outs, [], [*streams, gain.reshape(1, width)], 12, 1.8 * sets, "norm")


def pick(refs, at, layout, number):
    if len(refs) == 1:
        return refs[0][at]
    return jnp.where(layout.core() == number, refs[0][at], refs[1][at])


def low_rank(adapters, normed, down, layout, rank):
    sets, tokens, width = normed.shape
    arrays = [array for part in down for array in part.arrays]
    maps = down[0].rows

    def kernel(*refs):
        ids, x, refs, low = refs[: len(adapters)], refs[len(adapters)], refs[len(adapters) + 1 : -1], refs[-1]
        owner = layout.owner(maps, rank)
        part_width = width // len(down)
        blocks = ids[0].shape[1]
        rows = tokens // blocks
        for number in range(sets):
            total = 0.0
            at = 0
            for k, part in enumerate(down):
                own = refs[at : at + len(part.arrays)]
                at += len(part.arrays)
                columns = slice(k * part_width, (k + 1) * part_width)
                total = total + dot_t(x[number, :, columns], part.take(own, slice(None)))
            for block in range(blocks):
                here = slice(block * rows, (block + 1) * rows)
                match = owner == pick(ids, (0, block), layout, number)
                low[number, here] = jnp.where(match, total[here], 0.0).astype(jnp.bfloat16)

    return call(kernel, shape(sets, tokens, maps), adapters, [normed, *arrays], 12, 2.0, "low_rank")


def prompt_start(lengths, layout, number, token):
    start = jnp.zeros_like(token)
    bound = 0
    for prompt in range(lengths[0].shape[1] - 1):
        bound = bound + pick(lengths, (0, prompt), layout, number)
        start = jnp.where(token >= bound, bound, start)
    return start


def spans(tokens):
    return [min((i + 1) * STRIP, STRIP + BAND) for i in range(tokens // STRIP)]


def prompts(lengths, layout, tokens, head_width, taps):
    def kernel(*refs):
        lens, (reach, allowed) = refs[: len(lengths)], refs[len(lengths) :]
        for number in range(layout.sets):
            token = lax.broadcasted_iota(jnp.int32, (tokens, head_width), 0)
            since = token - prompt_start(lens, layout, number, token)
            for offset in range(1, taps):
                reach[number, offset - 1] = (since >= offset).astype(jnp.float32)
            for strip, span in enumerate(spans(tokens)):
                row = strip * STRIP + lax.broadcasted_iota(jnp.int32, (STRIP, span), 0)
                column = (strip + 1) * STRIP - span + lax.broadcasted_iota(jnp.int32, (STRIP, span), 1)
                inside = (column <= row) & (column >= prompt_start(lens, layout, number, row))
                allowed[number, strip, :, :span] = inside.astype(jnp.bfloat16)

    outs = [
        shape(layout.sets, taps - 1, tokens, head_width, dtype=jnp.float32),
        shape(layout.sets, tokens // STRIP, STRIP, STRIP + BAND),
    ]
    return call(kernel, outs, lengths, [], 8, 1.0 * layout.sets, "prompts")


def query_key(ordered, weights, first, columns):
    sets, tokens, _ = ordered.shape

    def kernel(x, *rest):
        refs, out = rest[:-1], rest[-1]
        side = weights.take(refs, slice(first, first + columns))
        for number in range(sets):
            out[number] = dot(x[number], side).astype(jnp.bfloat16)

    return call(kernel, shape(sets, tokens, columns), [], [ordered, *weights.arrays], 12, 1.3, "query_key")


def mixer(number, begin, group, ordered, qk, lows, taps, masks, weights, up, layout):
    _, tokens, width = ordered.shape
    head_width = width // HEADS
    features = qk.shape[2] // 2
    columns = group * head_width

    def kernel(x, qk, tap_table, reach, allowed, *rest):
        low_refs, rest = rest[: len(lows)], rest[len(lows) :]
        refs, rest = rest[: len(weights.arrays)], rest[len(weights.arrays) :]
        refs_up, out = rest[:-1], rest[-1]
        lane = lax.broadcasted_iota(jnp.int32, (tokens, features), 1) // QK
        ones = jnp.ones((max(spans(tokens)), head_width), jnp.bfloat16)
        here = slice(begin * head_width, begin * head_width + columns)
        first = layout.core() * (layout.heads * head_width) + begin * head_width
        v = dot(x[number], weights.take(refs, here))
        low = [ref[number] for ref in low_refs]
        low = low[0] if len(low) == 1 else jnp.concatenate(low, axis=1)
        delta = adapter_scale * dot(low, up.take(refs_up, here))
        v = v + delta.astype(jnp.bfloat16).astype(jnp.float32)
        tap = tap_table[:, pl.ds(pl.multiple_of(first, columns), columns)]
        conv = tap[0:1] * v
        for offset in range(1, taps.shape[0]):
            seen = jnp.concatenate([reach[number, offset - 1]] * group, axis=1)
            conv = conv + tap[offset : offset + 1] * (seen * pltpu.roll(v, offset, 0))
        mixed = (conv * (0.5 * v + 0.5 * v * jnp.tanh(0.5 * v))).astype(jnp.bfloat16)
        for part in range(group):
            query = qk[number, :, :features]
            query = jnp.where(lane == begin + part, query, jnp.zeros((), jnp.bfloat16))
            place = slice(part * head_width, (part + 1) * head_width)
            mine = mixed[:, place]
            for strip, span in enumerate(spans(tokens)):
                end = (strip + 1) * STRIP
                rows = slice(end - STRIP, end)
                near = slice(end - span, end)
                score = dot_t(query[rows], qk[number, near, features:]) + float(QK) ** 0.5
                weight = (score * score + float(QK)).astype(jnp.bfloat16)
                weight = weight * allowed[number, strip, :, :span]
                both = jnp.concatenate([mine[near], ones[:span]], axis=1)
                total = dot(weight, both)
                out[rows, place] = (total[:, :head_width] / total[:, head_width:]).astype(jnp.bfloat16)

    inputs = [ordered, qk, taps, *masks, *lows, *weights.arrays, *up.arrays]
    return call(kernel, shape(tokens, columns), [], inputs, 12, 1.2 * group, "mixer")


def arrange(pieces, layout):
    tokens, columns = pieces[0].shape
    width = columns * len(pieces)
    head_width = width // HEADS
    group = columns // head_width

    def kernel(*refs):
        out = refs[-1]
        core = layout.core()
        for number, piece in enumerate(refs[:-1]):
            side, local = divmod(number * group, layout.heads)
            owner = core if side == 0 else 1 - core
            for part in range(group):
                head = owner * layout.heads + local + part
                value = piece[:, part * head_width : (part + 1) * head_width].astype(jnp.float32)
                out[:, block_at(layout, head, head_width)] = layout.swap(value).astype(jnp.bfloat16)

    return call(kernel, shape(tokens, width), [], pieces, 12, 1.0, "arrange")


def project(bases, attended, weights, quarters, which, layout, dtype):
    tokens, width = attended[0].shape
    quarter = width // 4
    out_width = weights.arrays[0].shape[1]
    columns = 512
    inputs = [*attended, *weights.arrays, *bases]

    def kernel(*refs):
        x_refs, refs, out = refs[: len(attended)], refs[len(attended) : -1], refs[-1]
        w_refs, base_refs = refs[: len(weights.arrays)], refs[len(weights.arrays) :]

        def work(number):
            x = [x_refs[number][:, q * quarter : (q + 1) * quarter] for q in quarters]
            x = x[0] if len(x) == 1 else jnp.concatenate(x, axis=1)
            base = base_refs[0].at[which] if len(x_refs) == 1 else base_refs[number]
            for begin in range(0, out_width, columns):
                place = slice(begin, begin + columns)
                total = base[:, place].astype(jnp.float32) + dot(x, weights.take(w_refs, place))
                out[:, place] = total.astype(dtype)

        if len(attended) == 1:
            work(0)
        else:
            for number in range(2):
                pl.when(which(layout.core()) == number)(functools.partial(work, number))

    micros = 0.5 + 0.6 * len(quarters) * out_width / 1024
    return call(kernel, shape(tokens, out_width, dtype=dtype), [], inputs, 12, micros, "project")


def moves():
    def perm(to):
        pairs = []
        for z in range(4):
            for y in range(2):
                for x in range(2):
                    for c in range(2):
                        there = to(z, y, x, c)
                        target = ((there[0] * 2 + there[1]) * 2 + there[2]) * 2 + there[3]
                        pairs.append((((z * 2 + y) * 2 + x) * 2 + c, target))
        return pairs

    table = {
        "first": perm(lambda z, y, x, c: (z, y ^ c, x ^ (1 - c), c)),
        "last": perm(lambda z, y, x, c: (z, y ^ (1 - c), x ^ c, c)),
        "up": perm(lambda z, y, x, c: ((z + 1) % 4, y, x, c)),
        "down": perm(lambda z, y, x, c: ((z + 3) % 4, y, x, c)),
        "core": perm(lambda z, y, x, c: (z, y, x, 1 - c)),
    }
    return {name: functools.partial(lax.ppermute, axis_name=AXES, perm=p) for name, p in table.items()}


def after(value, *others):
    return lax.optimization_barrier((value, *others))[0]


def join(*parts):
    return jnp.concatenate(parts, axis=0)


def half_rows(picks, above_rows, layout, name):
    rows = picks[0][0].shape[0]
    widths = [columns // 2 for _, _, columns in picks]
    top = 0 if above_rows is None else above_rows.shape[0]
    arrays = [array for array, _, _ in picks] + ([] if above_rows is None else [above_rows])

    def kernel(*refs):
        out = refs[-1]
        if top:
            out[:top] = refs[-2][...]
        for number in range(2):

            @pl.when(layout.core() == number)
            def _():
                at = 0
                for source, (_, begin, columns) in zip(refs, picks):
                    half = columns // 2
                    there = slice(begin + number * half, begin + (number + 1) * half)
                    out[top:, at : at + half] = source[:, there]
                    at += half

    return call(kernel, shape(top + rows, sum(widths)), [], arrays, 8, 0.5, name)


def finish(kept, received, layout):
    tokens, half = kept.shape

    def kernel(here, there, out, arrived):
        for number in range(2):

            @pl.when(layout.core() == number)
            def _():
                sides = (here, there) if number == 0 else (there, here)
                copies = [
                    pltpu.make_async_copy(
                        side, out.at[:, k * half : (k + 1) * half], arrived.at[k]
                    )
                    for k, side in enumerate(sides)
                ]
                for copy in copies:
                    copy.start()
                for copy in copies:
                    copy.wait()

    return call(
        kernel,
        shape(tokens, 2 * half),
        [],
        [kept, received],
        8,
        1.0,
        "finish",
        scratch=[pltpu.SemaphoreType.DMA((2,))],
        out_specs=ANY,
    )


FLAGS = {'w1f': 0, 'w3f': 1, 'w2f': 0, 'o1': 1, 'o2': 1, 'o3': 1}
ORDER = {
    "w3": "v-far",
    "w0f": "qk-far",
    "l-far": "w0",
    "o-far": "w0 n-far l-far",
    "o0f": "w0f",
    "prompts": "n-far",
    "w0l": "df l-far o0f",
    "w2": "prompts",
    "w1f": "o-far",
    "dl": "o0f norm",
    "w13": "n-far o0f",
    "w3f": "w2 w1f",
    "w2f": "w0l",
    "o1": "w1f",
    "w13x": "dl",
    "o3": "w3f",
    "low": "o1",
    "low-far": "w13x",
    "o0l": "low",
    "o2": "o3",
    "o1l": "w2l",
    "o3l": "o0l",
    "qk": "low-far",
    "m00": "qk",
    "m04": "qk",
    "m00-far": "o1 o2",
    "m10": "o3 m04",
    "m14": "o2 m01-far",
    "m10-far": "qk",
    "m11-far": "m10",
    "e0": "m10",
    "e1": "a0 m14 a1",
}


def cube_local(
    stream,
    norm_weight,
    query_key_weight,
    value_weight,
    output_weight,
    convolution_weights,
    adapter_down_maps,
    adapter_up_maps,
    prompt_lengths,
    block_adapter_index,
):
    move = moves()
    first, last, above, below, swap = (move[n] for n in ("first", "last", "up", "down", "core"))
    tokens, width = stream.shape
    half = width // 2
    held, rank = adapter_down_maps.shape[:2]
    maps = held * rank
    features = HEADS * QK
    layout = CubeLayout(held)

    done = {}

    def do(name, work, value, *others):
        value = after(value, *[done[other] for other in ORDER.get(name, "").split()])
        result = work(value, *others)
        done[name] = result[0] if isinstance(result, (list, tuple)) else result
        return result

    def both(name, array):
        own = half_rows([(array, 0, width)], None, layout, name)
        return half_rows([(do(name + "-far", swap, array), 0, width)], own, layout, name)

    value_far = do("v-far", swap, value_weight)
    qk_far = do("qk-far", swap, query_key_weight)
    sides = [(0, features), (features, features)]
    parts = lambda v, qk: [(v, 0, width)] + [(qk, *side) for side in sides]
    w0 = half_rows(parts(value_weight, query_key_weight), None, layout, "own_half")
    w0 = half_rows(parts(value_far, qk_far), w0, layout, "far_half")
    done["w0"] = w0
    rows = w0.shape[0]
    w1, w3 = do("w1", above, w0), do("w3", below, w0)
    w0f = do("w0f", first, w0)
    up_halves = both("up", adapter_up_maps.reshape(maps, width))
    down_own = adapter_down_maps.reshape(maps, width)
    d0 = join(down_own[:, :half], down_own[:, half:], up_halves)
    df = do("df", first, d0)
    stream_far = do("s-far", swap, stream)
    numbers = block_adapter_index[None]
    adapters = [numbers, do("n-far", swap, numbers)]
    lengths = [prompt_lengths, do("l-far", swap, prompt_lengths)]
    o0 = both("o", output_weight)
    o0f = do("o0f", first, o0)
    masks = do(
        "prompts",
        lambda lens: prompts([lengths[0], lens], layout, tokens, width // HEADS, convolution_weights.shape[0]),
        lengths[1],
    )
    normed, ordered, base = do(
        "norm", lambda far: norm([stream, far], norm_weight, layout), stream_far
    )
    w = {"0": join(w0, w0f)}
    w["0l"] = do("w0l", last, w["0"])
    d = join(d0, df)
    w2 = do("w2", above, w1)
    w1f = do("w1f", above, w0f) if FLAGS["w1f"] else do("w1f", first, w1)
    dl = do("dl", last, d)
    w["13"] = do("w13", lambda value: join(value, w3), w1)
    w["13l"] = do("w13l", last, w["13"])
    w3f = do("w3f", below, w0f) if FLAGS["w3f"] else do("w3f", first, w3)
    w["2"] = join(w2, do("w2f", above, w1f) if FLAGS["w2f"] else do("w2f", first, w2))
    o = {"0": join(o0, o0f)}
    if FLAGS["o1"]:
        o["1"] = do("o1", above, o["0"])
    else:
        o1 = do("o1", above, o0)
        o["1"] = join(o1, do("o1f", first, o1))
    w["13f"] = join(w1f, w3f)
    w["13x"] = do("w13x", last, w["13f"])
    w["2l"] = do("w2l", last, w["2"])
    if FLAGS["o3"]:
        o["3"] = do("o3", below, o["0"])
    else:
        o3 = do("o3", below, o0)
        o["3"] = join(o3, do("o3f", first, o3))

    size = d0.shape[0]
    near = [(d, 0), (d, size), (dl, 0), (dl, size)]
    far = [near[0], near[2], near[1], near[3]]
    down = [Rows([(p, at + part * maps, maps) for p, at in near]) for part in range(2)]
    up = Rows([(p, at + 2 * maps, maps) for p, at in near] + [(p, at + 3 * maps, maps) for p, at in far])
    low = do("low", lambda x: low_rank(adapters, x, down, layout, rank), normed)
    lows = [low, do("low-far", swap, low)]
    o["0l"] = do("o0l", last, o["0"])
    if FLAGS["o2"]:
        o["2"] = do("o2", above, o["1"])
    else:
        o2 = do("o2", above, o["1"][:rows])
        o["2"] = join(o2, do("o2f", first, o2))
    o["1l"] = do("o1l", last, o["1"])
    o["3l"] = do("o3l", last, o["3"])
    o["2l"] = do("o2l", last, o["2"])

    places = [
        [("0", 0), ("0", rows), ("0l", 0), ("0l", rows)],
        [("13", 0), ("13f", 0), ("13l", 0), ("13x", 0)],
        [("2", 0), ("2", rows), ("2l", 0), ("2l", rows)],
        [("13", rows), ("13f", rows), ("13l", rows), ("13x", rows)],
    ]
    values = Rows([(w[p], at, rows) for step in places for p, at in step])
    qk = do("qk", lambda x: query_key(x, values, half, features), ordered)
    attended, early = [], []
    outs = [[(o[k + side], at, rows) for side in ("", "l") for at in (0, rows)] for k in "0123"]
    for number in range(2):
        pieces = []
        for begin in range(0, layout.heads, 4):
            name = f"m{number}{begin}"
            work = lambda x: mixer(
                number, begin, 4, x, qk, lows, convolution_weights, masks, values, up, layout
            )
            pieces.append(do(name, work, ordered))
        pieces += [do(f"m{number}{k}-far", swap, piece) for k, piece in enumerate(pieces)]
        attended.append(do(f"a{number}", lambda p: arrange([p, *pieces[1:]], layout), pieces[0]))
    soon = Rows(outs[0] + outs[1] + outs[3])
    for number in range(2):
        work = lambda a: project([base], [a], soon, (0, 1, 3), number, layout, jnp.float32)
        early.append(do(f"e{number}", work, attended[number]))
    late = Rows(outs[2])
    sent = project(early, attended, late, (2,), lambda core: 1 - core, layout, jnp.bfloat16)
    kept = project(early, attended, late, (2,), lambda core: core, layout, jnp.bfloat16)
    return finish(kept, swap(sent), layout)


def plain_local(
    stream,
    norm_weight,
    query_key_weight,
    value_weight,
    output_weight,
    convolution_weights,
    adapter_down_maps,
    adapter_up_maps,
    prompt_lengths,
    block_adapter_index,
):
    tokens, width = stream.shape
    gather = functools.partial(lax.all_gather, axis_name=AXES, axis=0, tiled=True)
    layout = Layout()
    normed, ordered, base = norm([stream], norm_weight, layout)
    masks = prompts([prompt_lengths], layout, tokens, width // HEADS, convolution_weights.shape[0])
    down = lax.all_gather(adapter_down_maps, "mp", axis=0, tiled=True)
    up = lax.all_gather(adapter_up_maps, "mp", axis=0, tiled=True)
    maps, rank = down.shape[0] * down.shape[1], down.shape[1]
    everything = lambda w: Rows([(w, 0, w.shape[0])])
    down, up = everything(down.reshape(maps, width)), everything(up.reshape(maps, width))
    low = low_rank([block_adapter_index[None]], normed, [down], layout, rank)
    qk = query_key(ordered, everything(gather(query_key_weight)), 0, 2 * HEADS * QK)
    values = everything(gather(value_weight))
    pieces = [
        mixer(0, begin, 4, ordered, qk, [low], convolution_weights, masks, values, up, layout)
        for begin in range(0, HEADS, 4)
    ]
    attended = arrange(pieces, layout)
    out = everything(gather(output_weight))
    return project([base], [attended], out, (0, 1, 2, 3), 0, layout, jnp.bfloat16)


def solution(mesh):
    cube = dict(mesh.shape) == {"dp": 4, "mp": 8}
    return jax.shard_map(
        cube_local if cube else plain_local,
        mesh=mesh,
        in_specs=(
            P(AXES, None),
            P(),
            P(AXES, None),
            P(AXES, None),
            P(AXES, None),
            P(),
            P("mp", None, None),
            P("mp", None, None),
            P(AXES, None),
            P(AXES),
        ),
        out_specs=P(AXES, None),
        check_vma=False,
    )
```

```python
import functools
import math

import jax
import jax.numpy as jnp
from jax import lax
from jax.experimental import pallas as pl
from jax.experimental.pallas import tpu as pltpu
from jax.sharding import PartitionSpec as P

HEADS = 16
QK = 16
BAND = 256
STRIP = 256
ROWS = 128
AXES = ("dp", "mp")

adapter_scale = 2.0
norm_eps = 1e-05

MIB = 1024 * 1024
VMEM = pl.BlockSpec(memory_space=pltpu.VMEM)
SMEM = pl.BlockSpec(memory_space=pltpu.SMEM)
ANY = pl.BlockSpec(memory_space=pl.ANY)


def params(mib):
    return pltpu.CompilerParams(vmem_limit_bytes=mib * MIB)


def cost(micros):
    return pl.CostEstimate(flops=int(micros * 1.1e9), bytes_accessed=0, transcendentals=0)


def dot(a, b):
    return jnp.dot(a, b, preferred_element_type=jnp.float32)


def dot_t(a, b):
    return lax.dot_general(a, b, (((1,), (1,)), ((), ())), preferred_element_type=jnp.float32)


class Rows:
    def __init__(self, pieces):
        self.arrays = []
        self.pieces = []
        for array, first, rows in pieces:
            known = [i for i, other in enumerate(self.arrays) if other is array]
            if not known:
                self.arrays.append(array)
                known = [len(self.arrays) - 1]
            self.pieces.append((known[0], first, rows))
        self.rows = sum(rows for _, _, rows in self.pieces)

    def take(self, refs, columns):
        parts = [refs[i][first : first + rows, columns] for i, first, rows in self.pieces]
        return parts[0] if len(parts) == 1 else jnp.concatenate(parts, axis=0)


class Layout:
    blocks = 16
    sets = 1
    heads = HEADS

    def core(self):
        return 0

    def place(self, block):
        return block

    def swap(self, value):
        return value

    def owner(self, count, rank):
        return lax.broadcasted_iota(jnp.int32, (1, count), 1) // rank


class CubeLayout(Layout):
    sets = 2
    heads = HEADS // 2

    def __init__(self, held):
        self.held = held

    def core(self):
        return lax.axis_index("mp") % 2

    def position(self):
        mp = lax.axis_index("mp")
        return lax.axis_index("dp"), mp // 4, (mp // 2) % 2, mp % 2

    def place(self, block):
        z, y, x, core = self.position()
        step = (z + 4 - block // 4) % 4
        off_y = lax.bitwise_xor(y, (block // 2) % 2)
        off_x = lax.bitwise_xor(x, block % 2)
        return step * 4 + off_y * (2 - core) + off_x * (1 + core)

    def swap(self, value):
        return jnp.where(self.core() != 0, pltpu.roll(value, value.shape[1] // 2, 1), value)

    def owner(self, count, rank):
        _, y, x, core = self.position()
        column = lax.broadcasted_iota(jnp.int32, (1, count), 1)
        maps = self.held * rank
        slot = column // maps
        to_first, to_last = slot % 2, slot // 2
        its_y = lax.bitwise_xor(y, jnp.where(core == 0, to_last, to_first))
        its_x = lax.bitwise_xor(x, jnp.where(core == 0, to_first, to_last))
        return (its_y * 4 + its_x * 2 + core) * self.held + (column % maps) // rank


def block_at(layout, block, width):
    return pl.ds(pl.multiple_of(layout.place(block) * width, width), width)


def shape(*dims, dtype=jnp.bfloat16):
    return jax.ShapeDtypeStruct(dims, dtype)


def call(kernel, outs, smem, vmem, mib, micros, name, scratch=(), out_specs=None, aliases=None):
    return pl.pallas_call(
        kernel,
        in_specs=[SMEM] * len(smem) + [VMEM] * len(vmem),
        out_specs=out_specs or jax.tree.map(lambda _: VMEM, outs),
        out_shape=outs,
        scratch_shapes=list(scratch),
        compiler_params=params(mib),
        cost_estimate=cost(micros),
        name=name,
    )(*smem, *vmem)


def norm(streams, gain, layout):
    sets = len(streams)
    tokens, width = streams[0].shape
    kept = width // sets
    block_width = width // layout.blocks

    def kernel(*refs):
        ins, weight, (normed, ordered, base) = refs[:sets], refs[sets], refs[sets + 1 :]
        core = layout.core()
        for number, source in enumerate(ins):
            at = 0 if sets == 1 else (core if number == 0 else 1 - core)

            @pl.loop(0, tokens // ROWS)
            def _(i):
                rows = pl.ds(pl.multiple_of(i * ROWS, ROWS), ROWS)
                x = source[rows].astype(jnp.float32)
                mean_sq = jnp.mean(x * x, axis=1, keepdims=True)
                y = x * lax.rsqrt(mean_sq + norm_eps) * weight[...]
                normed[at, rows] = y.astype(jnp.bfloat16)
                for block in range(layout.blocks):
                    part = y[:, block * block_width : (block + 1) * block_width]
                    place = block_at(layout, block, block_width)
                    ordered[at, rows, place] = layout.swap(part).astype(jnp.bfloat16)
                base[at, rows] = source[rows, pl.ds(pl.multiple_of(core * kept, kept), kept)]

    outs = [shape(sets, tokens, width), shape(sets, tokens, width), shape(sets, tokens, kept)]
    return call(kernel, outs, [], [*streams, gain.reshape(1, width)], 12, 1.8 * sets, "norm")


def pick(refs, at, layout, number):
    if len(refs) == 1:
        return refs[0][at]
    return jnp.where(layout.core() == number, refs[0][at], refs[1][at])


def low_rank(adapters, normed, down, layout, rank):
    sets, tokens, width = normed.shape
    arrays = [array for part in down for array in part.arrays]
    maps = down[0].rows

    def kernel(*refs):
        ids, x, refs, low = refs[: len(adapters)], refs[len(adapters)], refs[len(adapters) + 1 : -1], refs[-1]
        owner = layout.owner(maps, rank)
        part_width = width // len(down)
        blocks = ids[0].shape[1]
        rows = tokens // blocks
        for number in range(sets):
            total = 0.0
            at = 0
            for k, part in enumerate(down):
                own = refs[at : at + len(part.arrays)]
                at += len(part.arrays)
                columns = slice(k * part_width, (k + 1) * part_width)
                total = total + dot_t(x[number, :, columns], part.take(own, slice(None)))
            for block in range(blocks):
                here = slice(block * rows, (block + 1) * rows)
                match = owner == pick(ids, (0, block), layout, number)
                low[number, here] = jnp.where(match, total[here], 0.0).astype(jnp.bfloat16)

    return call(kernel, shape(sets, tokens, maps), adapters, [normed, *arrays], 12, 2.0, "low_rank")


def prompt_start(lengths, layout, number, token):
    start = jnp.zeros_like(token)
    bound = 0
    for prompt in range(lengths[0].shape[1] - 1):
        bound = bound + pick(lengths, (0, prompt), layout, number)
        start = jnp.where(token >= bound, bound, start)
    return start


def spans(tokens):
    return [min((i + 1) * STRIP, STRIP + BAND) for i in range(tokens // STRIP)]


def prompts(lengths, layout, tokens, head_width, taps):
    def kernel(*refs):
        lens, (reach, allowed) = refs[: len(lengths)], refs[len(lengths) :]
        for number in range(layout.sets):
            token = lax.broadcasted_iota(jnp.int32, (tokens, head_width), 0)
            since = token - prompt_start(lens, layout, number, token)
            for offset in range(1, taps):
                reach[number, offset - 1] = (since >= offset).astype(jnp.float32)
            for strip, span in enumerate(spans(tokens)):
                row = strip * STRIP + lax.broadcasted_iota(jnp.int32, (STRIP, span), 0)
                column = (strip + 1) * STRIP - span + lax.broadcasted_iota(jnp.int32, (STRIP, span), 1)
                inside = (column <= row) & (column >= prompt_start(lens, layout, number, row))
                allowed[number, strip, :, :span] = inside.astype(jnp.bfloat16)

    outs = [
        shape(layout.sets, taps - 1, tokens, head_width, dtype=jnp.float32),
        shape(layout.sets, tokens // STRIP, STRIP, STRIP + BAND),
    ]
    return call(kernel, outs, lengths, [], 8, 1.0 * layout.sets, "prompts")


def query_key(ordered, weights, first, columns):
    sets, tokens, _ = ordered.shape

    def kernel(x, *rest):
        refs, out = rest[:-1], rest[-1]
        side = weights.take(refs, slice(first, first + columns))
        for number in range(sets):
            out[number] = dot(x[number], side).astype(jnp.bfloat16)

    return call(kernel, shape(sets, tokens, columns), [], [ordered, *weights.arrays], 12, 1.3, "query_key")


def mixer(number, begin, group, ordered, qk, lows, taps, masks, weights, up, layout):
    _, tokens, width = ordered.shape
    head_width = width // HEADS
    features = qk.shape[2] // 2
    columns = group * head_width

    def kernel(x, qk, tap_table, reach, allowed, *rest):
        low_refs, rest = rest[: len(lows)], rest[len(lows) :]
        refs, rest = rest[: len(weights.arrays)], rest[len(weights.arrays) :]
        refs_up, out = rest[:-1], rest[-1]
        lane = lax.broadcasted_iota(jnp.int32, (tokens, features), 1) // QK
        ones = jnp.ones((max(spans(tokens)), head_width), jnp.bfloat16)
        here = slice(begin * head_width, begin * head_width + columns)
        first = layout.core() * (layout.heads * head_width) + begin * head_width
        v = dot(x[number], weights.take(refs, here))
        low = [ref[number] for ref in low_refs]
        low = low[0] if len(low) == 1 else jnp.concatenate(low, axis=1)
        delta = adapter_scale * dot(low, up.take(refs_up, here))
        v = v + delta.astype(jnp.bfloat16).astype(jnp.float32)
        tap = tap_table[:, pl.ds(pl.multiple_of(first, columns), columns)]
        conv = tap[0:1] * v
        for offset in range(1, taps.shape[0]):
            seen = jnp.concatenate([reach[number, offset - 1]] * group, axis=1)
            conv = conv + tap[offset : offset + 1] * (seen * pltpu.roll(v, offset, 0))
        mixed = (conv * (0.5 * v + 0.5 * v * jnp.tanh(0.5 * v))).astype(jnp.bfloat16)
        for part in range(group):
            query = qk[number, :, :features]
            query = jnp.where(lane == begin + part, query, jnp.zeros((), jnp.bfloat16))
            place = slice(part * head_width, (part + 1) * head_width)
            mine = mixed[:, place]
            for strip, span in enumerate(spans(tokens)):
                end = (strip + 1) * STRIP
                rows = slice(end - STRIP, end)
                near = slice(end - span, end)
                score = dot_t(query[rows], qk[number, near, features:]) + float(QK) ** 0.5
                weight = (score * score + float(QK)).astype(jnp.bfloat16)
                weight = weight * allowed[number, strip, :, :span]
                both = jnp.concatenate([mine[near], ones[:span]], axis=1)
                total = dot(weight, both)
                out[rows, place] = (total[:, :head_width] / total[:, head_width:]).astype(jnp.bfloat16)

    inputs = [ordered, qk, taps, *masks, *lows, *weights.arrays, *up.arrays]
    return call(kernel, shape(tokens, columns), [], inputs, 12, 1.2 * group, "mixer")


def arrange(pieces, layout):
    tokens, columns = pieces[0].shape
    width = columns * len(pieces)
    head_width = width // HEADS
    group = columns // head_width

    def kernel(*refs):
        out = refs[-1]
        core = layout.core()
        for number, piece in enumerate(refs[:-1]):
            side, local = divmod(number * group, layout.heads)
            owner = core if side == 0 else 1 - core
            for part in range(group):
                head = owner * layout.heads + local + part
                value = piece[:, part * head_width : (part + 1) * head_width].astype(jnp.float32)
                out[:, block_at(layout, head, head_width)] = layout.swap(value).astype(jnp.bfloat16)

    return call(kernel, shape(tokens, width), [], pieces, 12, 1.0, "arrange")


def project(bases, attended, weights, quarters, which, layout, dtype):
    tokens, width = attended[0].shape
    quarter = width // 4
    out_width = weights.arrays[0].shape[1]
    columns = 512
    inputs = [*attended, *weights.arrays, *bases]

    def kernel(*refs):
        x_refs, refs, out = refs[: len(attended)], refs[len(attended) : -1], refs[-1]
        w_refs, base_refs = refs[: len(weights.arrays)], refs[len(weights.arrays) :]

        def work(number):
            x = [x_refs[number][:, q * quarter : (q + 1) * quarter] for q in quarters]
            x = x[0] if len(x) == 1 else jnp.concatenate(x, axis=1)
            base = base_refs[0].at[which] if len(x_refs) == 1 else base_refs[number]
            for begin in range(0, out_width, columns):
                place = slice(begin, begin + columns)
                total = base[:, place].astype(jnp.float32) + dot(x, weights.take(w_refs, place))
                out[:, place] = total.astype(dtype)

        if len(attended) == 1:
            work(0)
        else:
            for number in range(2):
                pl.when(which(layout.core()) == number)(functools.partial(work, number))

    micros = 0.5 + 0.6 * len(quarters) * out_width / 1024
    return call(kernel, shape(tokens, out_width, dtype=dtype), [], inputs, 12, micros, "project")


def moves():
    def perm(to):
        pairs = []
        for z in range(4):
            for y in range(2):
                for x in range(2):
                    for c in range(2):
                        there = to(z, y, x, c)
                        target = ((there[0] * 2 + there[1]) * 2 + there[2]) * 2 + there[3]
                        pairs.append((((z * 2 + y) * 2 + x) * 2 + c, target))
        return pairs

    table = {
        "first": perm(lambda z, y, x, c: (z, y ^ c, x ^ (1 - c), c)),
        "last": perm(lambda z, y, x, c: (z, y ^ (1 - c), x ^ c, c)),
        "up": perm(lambda z, y, x, c: ((z + 1) % 4, y, x, c)),
        "down": perm(lambda z, y, x, c: ((z + 3) % 4, y, x, c)),
        "core": perm(lambda z, y, x, c: (z, y, x, 1 - c)),
    }
    return {name: functools.partial(lax.ppermute, axis_name=AXES, perm=p) for name, p in table.items()}


def after(value, *others):
    return lax.optimization_barrier((value, *others))[0]


def join(*parts):
    return jnp.concatenate(parts, axis=0)


def half_rows(picks, above_rows, layout, name):
    rows = picks[0][0].shape[0]
    widths = [columns // 2 for _, _, columns in picks]
    top = 0 if above_rows is None else above_rows.shape[0]
    arrays = [array for array, _, _ in picks] + ([] if above_rows is None else [above_rows])

    def kernel(*refs):
        out = refs[-1]
        if top:
            out[:top] = refs[-2][...]
        for number in range(2):

            @pl.when(layout.core() == number)
            def _():
                at = 0
                for source, (_, begin, columns) in zip(refs, picks):
                    half = columns // 2
                    there = slice(begin + number * half, begin + (number + 1) * half)
                    out[top:, at : at + half] = source[:, there]
                    at += half

    return call(kernel, shape(top + rows, sum(widths)), [], arrays, 8, 0.5, name)


def finish(kept, received, layout):
    tokens, half = kept.shape

    def kernel(here, there, out, arrived):
        for number in range(2):

            @pl.when(layout.core() == number)
            def _():
                sides = (here, there) if number == 0 else (there, here)
                copies = [
                    pltpu.make_async_copy(
                        side, out.at[:, k * half : (k + 1) * half], arrived.at[k]
                    )
                    for k, side in enumerate(sides)
                ]
                for copy in copies:
                    copy.start()
                for copy in copies:
                    copy.wait()

    return call(
        kernel,
        shape(tokens, 2 * half),
        [],
        [kept, received],
        8,
        1.0,
        "finish",
        scratch=[pltpu.SemaphoreType.DMA((2,))],
        out_specs=ANY,
    )


FLAGS = {'w1f': 0, 'w3f': 1, 'w2f': 0, 'o1': 1, 'o2': 1, 'o3': 1}
ORDER = {
    "w3": "v-far",
    "w0f": "qk-far",
    "l-far": "w0",
    "o-far": "w0 n-far l-far",
    "o0f": "w0f",
    "prompts": "n-far",
    "w0l": "df l-far o0f",
    "w2": "prompts",
    "w1f": "o-far",
    "dl": "o0f norm",
    "w13": "n-far o0f",
    "w3f": "w2 w1f",
    "w2f": "w0l",
    "o1": "w1f",
    "w13x": "dl",
    "o3": "w3f",
    "low": "o1",
    "low-far": "w13x",
    "o0l": "low",
    "o1l": "w2l",
    "qk": "low-far",
    "m00": "qk",
    "m04": "qk",
    "m00-far": "o1 o2",
    "m10": "o3 m04",
    "m14": "o2 m01-far",
    "m10-far": "qk",
    "m11-far": "m10",
    "e0": "m10",
    "e1": "a0 m14 a1",
}


def cube_local(
    stream,
    norm_weight,
    query_key_weight,
    value_weight,
    output_weight,
    convolution_weights,
    adapter_down_maps,
    adapter_up_maps,
    prompt_lengths,
    block_adapter_index,
):
    move = moves()
    first, last, above, below, swap = (move[n] for n in ("first", "last", "up", "down", "core"))
    tokens, width = stream.shape
    half = width // 2
    held, rank = adapter_down_maps.shape[:2]
    maps = held * rank
    features = HEADS * QK
    layout = CubeLayout(held)

    done = {}

    def do(name, work, value, *others):
        value = after(value, *[done[other] for other in ORDER.get(name, "").split()])
        result = work(value, *others)
        done[name] = result[0] if isinstance(result, (list, tuple)) else result
        return result

    def both(name, array):
        own = half_rows([(array, 0, width)], None, layout, name)
        return half_rows([(do(name + "-far", swap, array), 0, width)], own, layout, name)

    value_far = do("v-far", swap, value_weight)
    qk_far = do("qk-far", swap, query_key_weight)
    sides = [(0, features), (features, features)]
    parts = lambda v, qk: [(v, 0, width)] + [(qk, *side) for side in sides]
    w0 = half_rows(parts(value_weight, query_key_weight), None, layout, "own_half")
    w0 = half_rows(parts(value_far, qk_far), w0, layout, "far_half")
    done["w0"] = w0
    rows = w0.shape[0]
    w1, w3 = do("w1", above, w0), do("w3", below, w0)
    w0f = do("w0f", first, w0)
    up_halves = both("up", adapter_up_maps.reshape(maps, width))
    down_own = adapter_down_maps.reshape(maps, width)
    d0 = join(down_own[:, :half], down_own[:, half:], up_halves)
    df = do("df", first, d0)
    stream_far = do("s-far", swap, stream)
    numbers = block_adapter_index[None]
    adapters = [numbers, do("n-far", swap, numbers)]
    lengths = [prompt_lengths, do("l-far", swap, prompt_lengths)]
    o0 = both("o", output_weight)
    o0f = do("o0f", first, o0)
    masks = do(
        "prompts",
        lambda lens: prompts([lengths[0], lens], layout, tokens, width // HEADS, convolution_weights.shape[0]),
        lengths[1],
    )
    normed, ordered, base = do(
        "norm", lambda far: norm([stream, far], norm_weight, layout), stream_far
    )
    w = {"0": join(w0, w0f)}
    w["0l"] = do("w0l", last, w["0"])
    d = join(d0, df)
    w2 = do("w2", above, w1)
    w1f = do("w1f", above, w0f) if FLAGS["w1f"] else do("w1f", first, w1)
    dl = do("dl", last, d)
    w["13"] = do("w13", lambda value: join(value, w3), w1)
    w["13l"] = do("w13l", last, w["13"])
    w3f = do("w3f", below, w0f) if FLAGS["w3f"] else do("w3f", first, w3)
    w["2"] = join(w2, do("w2f", above, w1f) if FLAGS["w2f"] else do("w2f", first, w2))
    o = {"0": join(o0, o0f)}
    if FLAGS["o1"]:
        o["1"] = do("o1", above, o["0"])
    else:
        o1 = do("o1", above, o0)
        o["1"] = join(o1, do("o1f", first, o1))
    w["13f"] = join(w1f, w3f)
    w["13x"] = do("w13x", last, w["13f"])
    w["2l"] = do("w2l", last, w["2"])
    if FLAGS["o3"]:
        o["3"] = do("o3", below, o["0"])
    else:
        o3 = do("o3", below, o0)
        o["3"] = join(o3, do("o3f", first, o3))

    size = d0.shape[0]
    near = [(d, 0), (d, size), (dl, 0), (dl, size)]
    far = [near[0], near[2], near[1], near[3]]
    down = [Rows([(p, at + part * maps, maps) for p, at in near]) for part in range(2)]
    up = Rows([(p, at + 2 * maps, maps) for p, at in near] + [(p, at + 3 * maps, maps) for p, at in far])
    low = do("low", lambda x: low_rank(adapters, x, down, layout, rank), normed)
    lows = [low, do("low-far", swap, low)]
    o["0l"] = do("o0l", last, o["0"])
    if FLAGS["o2"]:
        o["2"] = do("o2", above, o["1"])
    else:
        o2 = do("o2", above, o["1"][:rows])
        o["2"] = join(o2, do("o2f", first, o2))
    o["1l"] = do("o1l", last, o["1"])
    o["3l"] = do("o3l", last, o["3"])
    o["2l"] = do("o2l", last, o["2"])

    places = [
        [("0", 0), ("0", rows), ("0l", 0), ("0l", rows)],
        [("13", 0), ("13f", 0), ("13l", 0), ("13x", 0)],
        [("2", 0), ("2", rows), ("2l", 0), ("2l", rows)],
        [("13", rows), ("13f", rows), ("13l", rows), ("13x", rows)],
    ]
    values = Rows([(w[p], at, rows) for step in places for p, at in step])
    qk = do("qk", lambda x: query_key(x, values, half, features), ordered)
    attended, early = [], []
    outs = [[(o[k + side], at, rows) for side in ("", "l") for at in (0, rows)] for k in "0123"]
    for number in range(2):
        pieces = []
        for begin in range(0, layout.heads, 4):
            name = f"m{number}{begin}"
            work = lambda x: mixer(
                number, begin, 4, x, qk, lows, convolution_weights, masks, values, up, layout
            )
            pieces.append(do(name, work, ordered))
        pieces += [do(f"m{number}{k}-far", swap, piece) for k, piece in enumerate(pieces)]
        attended.append(do(f"a{number}", lambda p: arrange([p, *pieces[1:]], layout), pieces[0]))
    soon = Rows(outs[0] + outs[1] + outs[3])
    for number in range(2):
        work = lambda a: project([base], [a], soon, (0, 1, 3), number, layout, jnp.float32)
        early.append(do(f"e{number}", work, attended[number]))
    late = Rows(outs[2])
    sent = project(early, attended, late, (2,), lambda core: 1 - core, layout, jnp.bfloat16)
    kept = project(early, attended, late, (2,), lambda core: core, layout, jnp.bfloat16)
    return finish(kept, swap(sent), layout)


def plain_local(
    stream,
    norm_weight,
    query_key_weight,
    value_weight,
    output_weight,
    convolution_weights,
    adapter_down_maps,
    adapter_up_maps,
    prompt_lengths,
    block_adapter_index,
):
    tokens, width = stream.shape
    gather = functools.partial(lax.all_gather, axis_name=AXES, axis=0, tiled=True)
    layout = Layout()
    normed, ordered, base = norm([stream], norm_weight, layout)
    masks = prompts([prompt_lengths], layout, tokens, width // HEADS, convolution_weights.shape[0])
    down = lax.all_gather(adapter_down_maps, "mp", axis=0, tiled=True)
    up = lax.all_gather(adapter_up_maps, "mp", axis=0, tiled=True)
    maps, rank = down.shape[0] * down.shape[1], down.shape[1]
    everything = lambda w: Rows([(w, 0, w.shape[0])])
    down, up = everything(down.reshape(maps, width)), everything(up.reshape(maps, width))
    low = low_rank([block_adapter_index[None]], normed, [down], layout, rank)
    qk = query_key(ordered, everything(gather(query_key_weight)), 0, 2 * HEADS * QK)
    values = everything(gather(value_weight))
    pieces = [
        mixer(0, begin, 4, ordered, qk, [low], convolution_weights, masks, values, up, layout)
        for begin in range(0, HEADS, 4)
    ]
    attended = arrange(pieces, layout)
    out = everything(gather(output_weight))
    return project([base], [attended], out, (0, 1, 2, 3), 0, layout, jnp.bfloat16)


def solution(mesh):
    cube = dict(mesh.shape) == {"dp": 4, "mp": 8}
    return jax.shard_map(
        cube_local if cube else plain_local,
        mesh=mesh,
        in_specs=(
            P(AXES, None),
            P(),
            P(AXES, None),
            P(AXES, None),
            P(AXES, None),
            P(),
            P("mp", None, None),
            P("mp", None, None),
            P(AXES, None),
            P(AXES),
        ),
        out_specs=P(AXES, None),
        check_vma=False,
    )
```
